128 devices in a mesh: grp: 4 (over x_lo, core), cond: 32 (over y, x_hi, z).
Axes of the slice: x: 4 (x_hi: 2, x_lo: 2; x = x_hi * 2 + x_lo), y: 4, z: 4, core: 2. Of those that a mesh axis runs over, the one named last changes fastest.
Arguments:
- valence_pairs: bfloat16 [64, 4096], P('grp', 'cond'), may hold values from -6 to 6
- screened: bfloat16 [4096, 4096], P('cond'), may hold values from -0.09375 to 0.09375
- cond_pairs: bfloat16 [262144, 4096], P(('grp', 'cond')), may hold values from -0.09375 to 0.09375
- owner_map: int32 [128, 32], P(('grp', 'cond')), may hold values from 0 to 31, as said below
- band_counts: int32 [128, 32], P(('grp', 'cond')), may hold values from 1 to 64, as said below
Outputs:
- owned_tiles: float32 [128, 32, 4096], P(('grp', 'cond'))
The draws below stay inside these ranges and needn't reach their ends.
Inputs may be any that keep to these rules, and one draw needn't show every extreme that they name: `owner_map`: each row is a permutation of 0 .. 31. `band_counts`: each row holds the value 64 at least once.
All inputs are finite; a program needn't handle non-finite values.
Results may differ from the reference program's by a relative error of at most 0.0029.
Values may be sent and summed in bfloat16 or wider, within the bound.
No kernel may reach another device: no remote copies, remote signals or barrier semaphores. Data moves between devices by JAX's collectives and lax.ppermute only.
A program may use at most 64 MiB of HBM per device.

```python
import jax
import jax.numpy as jnp

NV = 64
G = 4096
NCP = 262144
TILE_CP = 64
N_GRP = 4
N_COND = 32


def draw_owner_map(key, part):
    key = jax.random.fold_in(key, 11)
    keys = jax.random.split(key, N_GRP * N_COND)
    return jax.vmap(lambda k: jax.random.permutation(k, N_COND))(keys).astype(jnp.int32)


def draw_band_counts(key, part):
    key = jax.random.fold_in(key, 23)
    first, second = jax.random.split(key)
    counts = jax.random.randint(first, (N_GRP * N_COND, N_COND), 1, TILE_CP + 1)
    column = jax.random.randint(second, (N_GRP * N_COND, 1), 0, N_COND)
    places = jnp.arange(N_COND)[None, :]
    return jnp.where(places == column, TILE_CP, counts).astype(jnp.int32)


def block_scale(stream_key, shape, pieces, low, high):
    factor_of = 1.0
    for position, shards_of in pieces:
        draws = jax.random.uniform(jax.random.fold_in(jax.random.fold_in(stream_key, 6), position), (shards_of,), jnp.float32, low / len(pieces), high / len(pieces))
        factor_of = factor_of * jnp.repeat(jnp.exp(draws), shape[position] // shards_of).reshape((-1,) + (1,) * (len(shape) - 1 - position))
    return factor_of


def noise(key, extent, scale, limit, shards=(), kind=jnp.bfloat16):
    array = jax.random.normal(key, extent, jnp.float32) * scale
    if len(shards) > 0:
        array = block_scale(key, extent, shards, -0.22, 0.18) * array
    return jnp.clip(array, min=-limit, max=limit).astype(kind)


def setup_inputs(seed: int = 0) -> dict:
    key_of = jax.random.split(jax.random.key(seed), 6)
    return {
        "valence_pairs": noise(key_of[0], (NV, G), 1.0, 6.0, ((0, 4), (1, 32))),
        "screened": noise(key_of[1], (G, G), G ** -0.5, 0.09375, ((0, 32),)),
        "cond_pairs": noise(key_of[2], (NCP, G), G ** -0.5, 0.09375, ((0, 128),)),
        "owner_map": draw_owner_map(jax.random.fold_in(key_of[5], 71), 0),
        "band_counts": draw_band_counts(jax.random.fold_in(key_of[5], 71), 0),
    }


def reference(valence_pairs, screened, cond_pairs, owner_map, band_counts):
    projected = jnp.dot(valence_pairs, screened, preferred_element_type=jnp.float32).astype(jnp.bfloat16)
    kernel = jax.lax.dot_general(projected, cond_pairs, (((1,), (1,)), ((), ())), preferred_element_type=jnp.float32)
    devices = N_GRP * N_COND
    tiles = kernel.reshape(NV, devices, N_COND, TILE_CP).transpose(1, 2, 3, 0)
    rows = jnp.arange(TILE_CP, dtype=jnp.int32)
    keep = rows[None, None, :] < band_counts[:, :, None]
    tiles = jnp.where(keep[:, :, :, None], tiles, jnp.float32(0.0))
    inverse = jnp.argsort(owner_map, axis=1).astype(jnp.int32)
    chosen = jnp.take_along_axis(tiles, inverse[:, :, None, None], axis=1)
    chosen = chosen.reshape(N_GRP, N_COND, N_COND, TILE_CP * NV)
    owned_tiles = chosen.transpose(0, 2, 1, 3).reshape(devices, N_COND, TILE_CP * NV)
    return owned_tiles
```

```python
import jax
import jax.numpy as jnp
from jax import lax
from jax.sharding import PartitionSpec as P


def exchanged(x, axes):
    return lax.all_to_all(x, axes, split_axis=0, concat_axis=0, tiled=True)


def per_device(valence_pairs, screened, cond_pairs, owner_map, band_counts):
    groups = lax.axis_size("grp")
    ncond = lax.axis_size("cond")
    rows_dev = valence_pairs.shape[0]
    waves = screened.shape[1]
    piece = waves // ncond
    partial_sum = jnp.dot(valence_pairs, screened, preferred_element_type=jnp.float32)
    pieces = partial_sum.reshape(rows_dev, ncond, piece).transpose(1, 0, 2)
    mine = jnp.sum(exchanged(pieces, "cond"), axis=0).astype(jnp.bfloat16)
    copies = jnp.broadcast_to(mine, (groups * ncond, rows_dev, piece))
    everyone = exchanged(copies, ("grp", "cond"))
    projected = (
        everyone.reshape(groups, ncond, rows_dev, piece)
        .transpose(0, 2, 1, 3)
        .reshape(groups * rows_dev, waves)
    )
    kernel = lax.dot_general(
        cond_pairs, projected, (((1,), (1,)), ((), ())), preferred_element_type=jnp.float32
    )
    valence_all = groups * rows_dev
    tile_rows = cond_pairs.shape[0] // ncond
    tiles = kernel.reshape(ncond, tile_rows, valence_all)
    rows = jnp.arange(tile_rows, dtype=jnp.int32)
    keep = rows[None, :] < band_counts[0][:, None]
    tiles = jnp.where(keep[:, :, None], tiles, jnp.float32(0.0)).astype(jnp.bfloat16)
    tiles = tiles.reshape(ncond, tile_rows * valence_all)
    targets = jnp.arange(ncond, dtype=jnp.int32)
    selector = (owner_map[0][None, :] == targets[:, None]).astype(jnp.bfloat16)
    outgoing = jnp.dot(selector, tiles, preferred_element_type=jnp.float32).astype(jnp.bfloat16)
    lanes = 128
    arrived = exchanged(outgoing.reshape(ncond, -1, lanes), "cond")
    return arrived.astype(jnp.float32).reshape(1, ncond, tile_rows * valence_all)


def solution(mesh):
    return jax.shard_map(
        per_device,
        mesh=mesh,
        in_specs=(
            P("grp", "cond"),
            P("cond", None),
            P(("grp", "cond"), None),
            P(("grp", "cond"), None),
            P(("grp", "cond"), None),
        ),
        out_specs=P(("grp", "cond"), None, None),
        check_vma=False,
    )
```

```python
import functools

import jax
import jax.numpy as jnp
from jax import lax
from jax.experimental import pallas as pl
from jax.experimental.pallas import tpu as pltpu
from jax.sharding import PartitionSpec as P

LANES = 128
CORES = 2
VMEM = pl.BlockSpec(memory_space=pltpu.VMEM)
ANY = pl.BlockSpec(memory_space=pl.ANY)


def in_hbm(x):
    return pltpu.with_memory_space_constraint(x, pltpu.HBM)


def in_vmem(x):
    return pltpu.with_memory_space_constraint(x, pltpu.VMEM)


def exchanged(x, axes, groups=None):
    return lax.all_to_all(
        x, axes, split_axis=0, concat_axis=0, tiled=True, axis_index_groups=groups
    )


def from_other_core(x):
    count = lax.axis_size("grp")
    return lax.ppermute(x, "grp", [(i, i ^ 1) for i in range(count)])


def against(rows, other):
    return lax.dot_general(
        rows, other, (((1,), (1,)), ((), ())), preferred_element_type=jnp.float32
    )


def kernel_call(body, out_shape, in_specs, scratch=(), mib=16, flops=0, nbytes=0, name=None):
    return pl.pallas_call(
        body,
        out_shape=out_shape,
        in_specs=in_specs,
        out_specs=jax.tree.map(lambda _: VMEM, out_shape),
        scratch_shapes=scratch,
        compiler_params=pltpu.CompilerParams(vmem_limit_bytes=mib << 20),
        cost_estimate=pl.CostEstimate(flops=flops, bytes_accessed=nbytes, transcendentals=0),
        name=name,
    )


def load_body(count, *refs):
    sems = refs[-1]
    copies = [
        pltpu.make_async_copy(refs[i], refs[count + i], sems.at[i]) for i in range(count)
    ]
    for copy in copies:
        copy.start()
    for copy in copies:
        copy.wait()


def loaded(name, *arrays):
    return kernel_call(
        functools.partial(load_body, len(arrays)),
        [pltpu.VMEM(x.shape, x.dtype) for x in arrays],
        [ANY] * len(arrays),
        scratch=[pltpu.SemaphoreType.DMA((len(arrays),))],
        nbytes=sum(2 * x.size * x.dtype.itemsize for x in arrays),
        name=name,
    )(*[in_hbm(x) for x in arrays])


def partial_body(own_ref, other_ref, screened_ref, out_ref):
    core = lax.axis_index("grp") % CORES
    width = screened_ref.shape[1] // CORES
    half = screened_ref[:, pl.ds(pl.multiple_of(core * width, width), width)]
    rows_dev = own_ref.shape[0]
    own = jnp.dot(own_ref[...], half, preferred_element_type=jnp.float32)
    other = jnp.dot(other_ref[...], half, preferred_element_type=jnp.float32)
    for t in range(width // LANES):
        lanes = slice(t * LANES, (t + 1) * LANES)
        out_ref[CORES * t + core] = own[:, lanes]
        out_ref[CORES * t + (1 - core)] = other[:, lanes]


def sum_body(pieces_ref, cond_ref, out_ref):
    total = pieces_ref[0]
    for c in range(1, pieces_ref.shape[0]):
        total = total + pieces_ref[c]
    rounded = total.astype(jnp.bfloat16)
    for d in range(out_ref.shape[0]):
        out_ref[d] = rounded


def half_of(own_half, cond_ref):
    core = lax.axis_index("grp") % CORES
    which = core if own_half else 1 - core
    width = cond_ref.shape[1] // CORES
    return cond_ref[:, pl.ds(pl.multiple_of(which * width, width), width)]


def assemble(groups, pieces_ref, projected):
    ncond = pieces_ref.shape[0] * CORES // groups
    rows_dev = pieces_ref.shape[1]
    valence_all = groups * rows_dev
    for d in range(pieces_ref.shape[0]):
        c = d % ncond
        group = CORES * (d // ncond) + c % CORES
        lanes = slice(c // CORES * LANES, (c // CORES + 1) * LANES)
        piece = pieces_ref[d]
        for start in (group * rows_dev, valence_all + group * rows_dev):
            projected[start : start + rows_dev, lanes] = piece


def first_body(groups, pieces_ref, cond_ref, out_ref, projected):
    assemble(groups, pieces_ref, projected)
    out_ref[...] = against(half_of(True, cond_ref), projected[...])


def tiles_body(
    groups, pieces_ref, cond_ref, first_ref, owner_ref, counts_ref, out_ref,
    projected, product, owner, counts, sems,
):
    loads = [
        pltpu.make_async_copy(owner_ref, owner, sems.at[0]),
        pltpu.make_async_copy(counts_ref, counts, sems.at[1]),
    ]
    for load in loads:
        load.start()
    assemble(groups, pieces_ref, projected)
    product[...] = first_ref[...] + against(half_of(False, cond_ref), projected[...])
    for load in loads:
        load.wait()
    ncond, pairs, _ = out_ref.shape
    tile_rows = 2 * pairs
    lane = lax.broadcasted_iota(jnp.int32, (pairs, LANES), 1)
    second = lane >= LANES // 2
    place = 2 * lax.broadcasted_iota(jnp.int32, (pairs, LANES), 0) + second.astype(jnp.int32)
    for j in range(ncond):
        even = product[pl.ds(tile_rows * j, pairs, stride=2), :]
        odd = product[pl.ds(tile_rows * j + 1, pairs, stride=2), :]
        tile = jnp.where(second, odd, even)
        tile = jnp.where(place < counts[0, j], tile, jnp.float32(0.0))
        out_ref[owner[0, j]] = tile.astype(jnp.bfloat16)


def widen_body(tiles_ref, out_ref, wide):
    wide[...] = tiles_ref[...].astype(jnp.float32)
    for l in range(tiles_ref.shape[1]):
        out_ref[0, :, l * LANES : (l + 1) * LANES] = wide[:, l, :]


def per_device(valence_pairs, screened, cond_pairs, owner_map, band_counts):
    groups = lax.axis_size("grp")
    ncond = lax.axis_size("cond")
    rows_dev = valence_pairs.shape[0]
    waves = screened.shape[1]
    pairs_dev = cond_pairs.shape[0]
    valence_all = groups * rows_dev
    tile_size = pairs_dev // ncond * valence_all
    pairs = tile_size // LANES
    same_core = [
        [g * ncond + c for g in range(core, groups, CORES) for c in range(ncond)]
        for core in range(CORES)
    ]

    own, screened_vmem = loaded("load_first", valence_pairs, screened)
    pieces = kernel_call(
        partial_body,
        jax.ShapeDtypeStruct((ncond, rows_dev, LANES), jnp.float32),
        [VMEM, VMEM, VMEM],
        flops=2 * rows_dev * screened.shape[0] * waves,
        nbytes=2 * screened.size,
        name="partial",
    )(
        in_vmem(own), from_other_core(valence_pairs), in_vmem(screened_vmem)
    )
    arrived = exchanged(pieces, "cond")
    copies = kernel_call(
        sum_body,
        jax.ShapeDtypeStruct((len(same_core[0]), rows_dev, LANES), jnp.bfloat16),
        [VMEM, ANY],
        nbytes=arrived.size * 4,
        name="sum_pieces",
    )(arrived, in_hbm(cond_pairs))
    gathered = exchanged(copies, ("grp", "cond"), same_core)
    others = from_other_core(gathered)
    half_scratch = [pltpu.VMEM((2 * valence_all, waves // CORES), jnp.bfloat16)]
    first = kernel_call(
        functools.partial(first_body, groups),
        jax.ShapeDtypeStruct((pairs_dev, LANES), jnp.float32),
        [VMEM, VMEM],
        scratch=half_scratch,
        flops=pairs_dev * waves * valence_all,
        nbytes=cond_pairs.size,
        name="first_half",
    )(gathered, cond_pairs)
    outgoing = kernel_call(
        functools.partial(tiles_body, groups),
        jax.ShapeDtypeStruct((ncond, pairs, LANES), jnp.bfloat16),
        [VMEM, VMEM, VMEM, ANY, ANY],
        scratch=[
            *half_scratch,
            pltpu.VMEM((pairs_dev, LANES), jnp.float32),
            pltpu.SMEM((1, ncond), jnp.int32),
            pltpu.SMEM((1, ncond), jnp.int32),
            pltpu.SemaphoreType.DMA((2,)),
        ],
        flops=pairs_dev * waves * valence_all,
        nbytes=cond_pairs.size,
        name="tiles",
    )(others, cond_pairs, first, in_hbm(owner_map), in_hbm(band_counts))
    tiles = exchanged(outgoing, "cond")
    return kernel_call(
        widen_body,
        jax.ShapeDtypeStruct((1, ncond, tile_size), jnp.float32),
        [VMEM],
        scratch=[pltpu.VMEM((ncond, pairs, LANES), jnp.float32)],
        nbytes=6 * ncond * tile_size,
        name="widen",
    )(tiles)


def solution(mesh):
    return jax.shard_map(
        per_device,
        mesh=mesh,
        in_specs=(
            P("grp", "cond"),
            P("cond", None),
            P(("grp", "cond"), None),
            P(("grp", "cond"), None),
            P(("grp", "cond"), None),
        ),
        out_specs=P(("grp", "cond"), None, None),
        check_vma=False,
    )
```

```python
import functools

import jax
import jax.numpy as jnp
from jax import lax
from jax.experimental import pallas as pl
from jax.experimental.pallas import tpu as pltpu
from jax.sharding import PartitionSpec as P

LANES = 128
CORES = 2
VMEM = pl.BlockSpec(memory_space=pltpu.VMEM)
ANY = pl.BlockSpec(memory_space=pl.ANY)


def in_hbm(x):
    return pltpu.with_memory_space_constraint(x, pltpu.HBM)


def in_vmem(x):
    return pltpu.with_memory_space_constraint(x, pltpu.VMEM)


def exchanged(x, axes, groups=None):
    return lax.all_to_all(
        x, axes, split_axis=0, concat_axis=0, tiled=True, axis_index_groups=groups
    )


def from_other_core(x):
    count = lax.axis_size("grp")
    return lax.ppermute(x, "grp", [(i, i ^ 1) for i in range(count)])


def against(rows, other):
    return lax.dot_general(
        rows, other, (((1,), (1,)), ((), ())), preferred_element_type=jnp.float32
    )


def kernel_call(body, out_shape, in_specs, scratch=(), mib=16, flops=0, nbytes=0, out_space=VMEM, name=None):
    return pl.pallas_call(
        body,
        out_shape=out_shape,
        in_specs=in_specs,
        out_specs=jax.tree.map(lambda _: out_space, out_shape),
        scratch_shapes=scratch,
        compiler_params=pltpu.CompilerParams(vmem_limit_bytes=mib << 20),
        cost_estimate=pl.CostEstimate(flops=flops, bytes_accessed=nbytes, transcendentals=0),
        name=name,
    )


def core_half(own_half, width):
    core = lax.axis_index("grp") % CORES
    which = core if own_half else 1 - core
    return pl.ds(pl.multiple_of(which * width, width), width)


def load_body(valence_hbm, screened_hbm, valence_ref, screened_ref, sems):
    lanes = core_half(True, screened_ref.shape[1])
    copies = [
        pltpu.make_async_copy(screened_hbm.at[:, lanes], screened_ref, sems.at[0]),
        pltpu.make_async_copy(valence_hbm, valence_ref, sems.at[1]),
    ]
    for copy in copies:
        copy.start()
    for copy in copies:
        copy.wait()


def partial_body(own_ref, other_ref, screened_ref, out_ref):
    core = lax.axis_index("grp") % CORES
    half = screened_ref[...]
    own = jnp.dot(own_ref[...], half, preferred_element_type=jnp.float32)
    other = jnp.dot(other_ref[...], half, preferred_element_type=jnp.float32)
    for t in range(half.shape[1] // LANES):
        lanes = slice(t * LANES, (t + 1) * LANES)
        out_ref[CORES * t + core] = own[:, lanes]
        out_ref[CORES * t + (1 - core)] = other[:, lanes]


def sum_body(pieces_ref, cond_ref, out_ref):
    total = pieces_ref[0]
    for c in range(1, pieces_ref.shape[0]):
        total = total + pieces_ref[c]
    rounded = total.astype(jnp.bfloat16)
    for d in range(out_ref.shape[0]):
        out_ref[d] = rounded


def half_of(own_half, cond_ref):
    return cond_ref[:, core_half(own_half, cond_ref.shape[1] // CORES)]


def assemble(groups, pieces_ref, projected):
    ncond = pieces_ref.shape[0] * CORES // groups
    rows_dev = pieces_ref.shape[1]
    valence_all = groups * rows_dev
    for d in range(pieces_ref.shape[0]):
        c = d % ncond
        group = CORES * (d // ncond) + c % CORES
        lanes = slice(c // CORES * LANES, (c // CORES + 1) * LANES)
        piece = pieces_ref[d]
        for start in (group * rows_dev, valence_all + group * rows_dev):
            projected[start : start + rows_dev, lanes] = piece


def first_body(groups, pieces_ref, cond_ref, out_ref, projected):
    assemble(groups, pieces_ref, projected)
    out_ref[...] = against(half_of(True, cond_ref), projected[...])


def tiles_body(
    groups, pieces_ref, cond_ref, first_ref, owner_ref, counts_ref, out_ref,
    projected, product, owner, counts, sems,
):
    loads = [
        pltpu.make_async_copy(owner_ref, owner, sems.at[0]),
        pltpu.make_async_copy(counts_ref, counts, sems.at[1]),
    ]
    for load in loads:
        load.start()
    assemble(groups, pieces_ref, projected)
    product[...] = first_ref[...] + against(half_of(False, cond_ref), projected[...])
    for load in loads:
        load.wait()
    ncond, pairs, _ = out_ref.shape
    tile_rows = 2 * pairs
    lane = lax.broadcasted_iota(jnp.int32, (pairs, LANES), 1)
    second = lane >= LANES // 2
    place = 2 * lax.broadcasted_iota(jnp.int32, (pairs, LANES), 0) + second.astype(jnp.int32)
    for j in range(ncond):
        even = product[pl.ds(tile_rows * j, pairs, stride=2), :]
        odd = product[pl.ds(tile_rows * j + 1, pairs, stride=2), :]
        tile = jnp.where(second, odd, even)
        tile = jnp.where(place < counts[0, j], tile, jnp.float32(0.0))
        out_ref[owner[0, j]] = tile.astype(jnp.bfloat16)


def widen_body(tiles_ref, out_ref, wide, sems):
    count, pairs, lanes = tiles_ref.shape
    copies = []
    for i in range(sems.shape[0]):
        rows = slice(i * count // sems.shape[0], (i + 1) * count // sems.shape[0])
        tiles = tiles_ref[rows].astype(jnp.float32)
        wide[rows, :] = tiles.reshape(tiles.shape[0], pairs * lanes)
        copies.append(
            pltpu.make_async_copy(wide.at[rows, :], out_ref.at[0, rows, :], sems.at[i])
        )
        copies[-1].start()
    for copy in copies:
        copy.wait()


def per_device(valence_pairs, screened, cond_pairs, owner_map, band_counts):
    groups = lax.axis_size("grp")
    ncond = lax.axis_size("cond")
    rows_dev = valence_pairs.shape[0]
    waves = screened.shape[1]
    pairs_dev = cond_pairs.shape[0]
    valence_all = groups * rows_dev
    tile_size = pairs_dev // ncond * valence_all
    pairs = tile_size // LANES
    same_core = [
        [g * ncond + c for g in range(core, groups, CORES) for c in range(ncond)]
        for core in range(CORES)
    ]

    own, screened_half = kernel_call(
        load_body,
        [
            pltpu.VMEM(valence_pairs.shape, valence_pairs.dtype),
            pltpu.VMEM((screened.shape[0], waves // CORES), screened.dtype),
        ],
        [ANY, ANY],
        scratch=[pltpu.SemaphoreType.DMA((2,))],
        nbytes=2 * screened.size,
        name="load_first",
    )(in_hbm(valence_pairs), in_hbm(screened))
    pieces = kernel_call(
        partial_body,
        jax.ShapeDtypeStruct((ncond, rows_dev, LANES), jnp.float32),
        [VMEM, VMEM, VMEM],
        flops=2 * rows_dev * screened.shape[0] * waves,
        nbytes=2 * screened.size,
        name="partial",
    )(
        in_vmem(own), from_other_core(valence_pairs), in_vmem(screened_half)
    )
    arrived = exchanged(pieces, "cond")
    copies = kernel_call(
        sum_body,
        jax.ShapeDtypeStruct((len(same_core[0]), rows_dev, LANES), jnp.bfloat16),
        [VMEM, ANY],
        nbytes=arrived.size * 4,
        name="sum_pieces",
    )(arrived, in_hbm(cond_pairs))
    gathered = exchanged(copies, ("grp", "cond"), same_core)
    others = from_other_core(gathered)
    half_scratch = [pltpu.VMEM((2 * valence_all, waves // CORES), jnp.bfloat16)]
    first = kernel_call(
        functools.partial(first_body, groups),
        jax.ShapeDtypeStruct((pairs_dev, LANES), jnp.float32),
        [VMEM, VMEM],
        scratch=half_scratch,
        flops=pairs_dev * waves * valence_all,
        nbytes=cond_pairs.size,
        name="first_half",
    )(gathered, cond_pairs)
    outgoing = kernel_call(
        functools.partial(tiles_body, groups),
        jax.ShapeDtypeStruct((ncond, pairs, LANES), jnp.bfloat16),
        [VMEM, VMEM, VMEM, ANY, ANY],
        scratch=[
            *half_scratch,
            pltpu.VMEM((pairs_dev, LANES), jnp.float32),
            pltpu.SMEM((1, ncond), jnp.int32),
            pltpu.SMEM((1, ncond), jnp.int32),
            pltpu.SemaphoreType.DMA((2,)),
        ],
        flops=pairs_dev * waves * valence_all,
        nbytes=cond_pairs.size,
        name="tiles",
    )(others, cond_pairs, first, in_hbm(owner_map), in_hbm(band_counts))
    tiles = exchanged(outgoing, "cond")
    return kernel_call(
        widen_body,
        jax.ShapeDtypeStruct((1, ncond, tile_size), jnp.float32),
        [VMEM],
        scratch=[
            pltpu.VMEM((ncond, tile_size), jnp.float32),
            pltpu.SemaphoreType.DMA((4,)),
        ],
        nbytes=6 * ncond * tile_size,
        out_space=ANY,
        name="widen",
    )(tiles)


def solution(mesh):
    return jax.shard_map(
        per_device,
        mesh=mesh,
        in_specs=(
            P("grp", "cond"),
            P("cond", None),
            P(("grp", "cond"), None),
            P(("grp", "cond"), None),
            P(("grp", "cond"), None),
        ),
        out_specs=P(("grp", "cond"), None, None),
        check_vma=False,
    )
```

```python
import functools

import jax
import jax.numpy as jnp
from jax import lax
from jax.experimental import pallas as pl
from jax.experimental.pallas import tpu as pltpu
from jax.sharding import PartitionSpec as P

LANES = 128
CORES = 2
SPARE_ROWS = 8
VMEM = pl.BlockSpec(memory_space=pltpu.VMEM)
ANY = pl.BlockSpec(memory_space=pl.ANY)


def in_hbm(x):
    return pltpu.with_memory_space_constraint(x, pltpu.HBM)


def in_vmem(x):
    return pltpu.with_memory_space_constraint(x, pltpu.VMEM)


def exchanged(x, axes, groups=None):
    return lax.all_to_all(
        x, axes, split_axis=0, concat_axis=0, tiled=True, axis_index_groups=groups
    )


def from_other_core(x):
    count = lax.axis_size("grp")
    return lax.ppermute(x, "grp", [(i, i ^ 1) for i in range(count)])


def against(rows, other):
    return lax.dot_general(
        rows, other, (((1,), (1,)), ((), ())), preferred_element_type=jnp.float32
    )


def kernel_call(body, out_shape, in_specs, scratch=(), mib=16, flops=0, nbytes=0, out_space=VMEM, name=None):
    return pl.pallas_call(
        body,
        out_shape=out_shape,
        in_specs=in_specs,
        out_specs=jax.tree.map(lambda _: out_space, out_shape),
        scratch_shapes=scratch,
        compiler_params=pltpu.CompilerParams(vmem_limit_bytes=mib << 20),
        cost_estimate=pl.CostEstimate(flops=flops, bytes_accessed=nbytes, transcendentals=0),
        name=name,
    )


def core_half(own_half, width):
    core = lax.axis_index("grp") % CORES
    which = core if own_half else 1 - core
    return pl.ds(pl.multiple_of(which * width, width), width)


def load_body(valence_hbm, screened_hbm, valence_ref, screened_ref, sems):
    lanes = core_half(True, screened_ref.shape[1])
    copies = [
        pltpu.make_async_copy(screened_hbm.at[:, lanes], screened_ref, sems.at[0]),
        pltpu.make_async_copy(valence_hbm, valence_ref, sems.at[1]),
    ]
    for copy in copies:
        copy.start()
    for copy in copies:
        copy.wait()


def partial_body(own_ref, other_ref, screened_ref, out_ref):
    core = lax.axis_index("grp") % CORES
    half = screened_ref[...]
    rows = jnp.concatenate([own_ref[...], other_ref[...]], axis=0)
    both = jnp.dot(rows, half, preferred_element_type=jnp.float32)
    own, other = both[: own_ref.shape[0]], both[own_ref.shape[0] :]
    for t in range(half.shape[1] // LANES):
        lanes = slice(t * LANES, (t + 1) * LANES)
        out_ref[CORES * t + core] = own[:, lanes]
        out_ref[CORES * t + (1 - core)] = other[:, lanes]


def sum_body(pieces_ref, cond_ref, out_ref):
    total = pieces_ref[0]
    for c in range(1, pieces_ref.shape[0]):
        total = total + pieces_ref[c]
    rounded = total.astype(jnp.bfloat16)
    for d in range(out_ref.shape[0]):
        out_ref[d] = rounded


def half_of(own_half, cond_ref):
    return cond_ref[:, core_half(own_half, cond_ref.shape[1] // CORES)]


def assemble(groups, pieces_ref, projected):
    ncond = pieces_ref.shape[0] * CORES // groups
    rows_dev = pieces_ref.shape[1]
    valence_all = groups * rows_dev
    for d in range(pieces_ref.shape[0]):
        c = d % ncond
        group = CORES * (d // ncond) + c % CORES
        lanes = slice(c // CORES * LANES, (c // CORES + 1) * LANES)
        piece = pieces_ref[d]
        for start in (group * rows_dev, valence_all + group * rows_dev):
            projected[start : start + rows_dev, lanes] = piece


def first_body(groups, pieces_ref, cond_ref, out_ref, projected):
    assemble(groups, pieces_ref, projected)
    out_ref[...] = against(half_of(True, cond_ref), projected[...])


def tiles_body(
    groups, pieces_ref, cond_ref, first_ref, owner_ref, counts_ref, out_ref,
    projected, product, owner, counts, sems,
):
    loads = [
        pltpu.make_async_copy(owner_ref, owner, sems.at[0]),
        pltpu.make_async_copy(counts_ref, counts, sems.at[1]),
    ]
    for load in loads:
        load.start()
    assemble(groups, pieces_ref, projected)
    product[0 : first_ref.shape[0], :] = first_ref[...] + against(
        half_of(False, cond_ref), projected[...]
    )
    for load in loads:
        load.wait()
    ncond, pairs, _ = out_ref.shape
    tile_rows = 2 * pairs
    lane = lax.broadcasted_iota(jnp.int32, (pairs, LANES), 1)
    second = lane >= LANES // 2
    place = 2 * lax.broadcasted_iota(jnp.int32, (pairs, LANES), 0) + second.astype(jnp.int32)
    for j in range(ncond):
        even = product[pl.ds(tile_rows * j, pairs, stride=2), :]
        odd = product[pl.ds(tile_rows * j + 1, pairs, stride=2), :]
        tile = jnp.where(second, odd, even)
        tile = jnp.where(place < counts[0, j], tile, jnp.float32(0.0))
        out_ref[owner[0, j]] = tile.astype(jnp.bfloat16)


def widen_body(tiles_ref, out_ref, wide, sems):
    count, pairs, lanes = tiles_ref.shape
    copies = []
    for i in range(sems.shape[0]):
        rows = slice(i * count // sems.shape[0], (i + 1) * count // sems.shape[0])
        tiles = tiles_ref[rows].astype(jnp.float32)
        wide[rows, :] = tiles.reshape(tiles.shape[0], pairs * lanes)
        copies.append(
            pltpu.make_async_copy(wide.at[rows, :], out_ref.at[0, rows, :], sems.at[i])
        )
        copies[-1].start()
    for copy in copies:
        copy.wait()


def per_device(valence_pairs, screened, cond_pairs, owner_map, band_counts):
    groups = lax.axis_size("grp")
    ncond = lax.axis_size("cond")
    rows_dev = valence_pairs.shape[0]
    waves = screened.shape[1]
    pairs_dev = cond_pairs.shape[0]
    valence_all = groups * rows_dev
    tile_size = pairs_dev // ncond * valence_all
    pairs = tile_size // LANES
    same_core = [
        [g * ncond + c for g in range(core, groups, CORES) for c in range(ncond)]
        for core in range(CORES)
    ]

    own, screened_half = kernel_call(
        load_body,
        [
            pltpu.VMEM(valence_pairs.shape, valence_pairs.dtype),
            pltpu.VMEM((screened.shape[0], waves // CORES), screened.dtype),
        ],
        [ANY, ANY],
        scratch=[pltpu.SemaphoreType.DMA((2,))],
        nbytes=2 * screened.size,
        name="load_first",
    )(in_hbm(valence_pairs), in_hbm(screened))
    pieces = kernel_call(
        partial_body,
        jax.ShapeDtypeStruct((ncond, rows_dev, LANES), jnp.float32),
        [VMEM, VMEM, VMEM],
        flops=2 * rows_dev * screened.shape[0] * waves,
        nbytes=2 * screened.size,
        name="partial",
    )(
        in_vmem(own), from_other_core(valence_pairs), in_vmem(screened_half)
    )
    arrived = exchanged(pieces, "cond")
    copies = kernel_call(
        sum_body,
        jax.ShapeDtypeStruct((len(same_core[0]), rows_dev, LANES), jnp.bfloat16),
        [VMEM, ANY],
        nbytes=arrived.size * 4,
        name="sum_pieces",
    )(arrived, in_hbm(cond_pairs))
    gathered = exchanged(copies, ("grp", "cond"), same_core)
    others = from_other_core(gathered)
    half_scratch = [pltpu.VMEM((2 * valence_all, waves // CORES), jnp.bfloat16)]
    first = kernel_call(
        functools.partial(first_body, groups),
        jax.ShapeDtypeStruct((pairs_dev, LANES), jnp.float32),
        [VMEM, VMEM],
        scratch=half_scratch,
        flops=pairs_dev * waves * valence_all,
        nbytes=cond_pairs.size,
        name="first_half",
    )(gathered, cond_pairs)
    outgoing = kernel_call(
        functools.partial(tiles_body, groups),
        jax.ShapeDtypeStruct((ncond, pairs, LANES), jnp.bfloat16),
        [VMEM, VMEM, VMEM, ANY, ANY],
        scratch=[
            *half_scratch,
            pltpu.VMEM((pairs_dev + SPARE_ROWS, LANES), jnp.float32),
            pltpu.SMEM((1, ncond), jnp.int32),
            pltpu.SMEM((1, ncond), jnp.int32),
            pltpu.SemaphoreType.DMA((2,)),
        ],
        flops=pairs_dev * waves * valence_all,
        nbytes=cond_pairs.size,
        name="tiles",
    )(others, cond_pairs, first, in_hbm(owner_map), in_hbm(band_counts))
    tiles = exchanged(outgoing, "cond")
    return kernel_call(
        widen_body,
        jax.ShapeDtypeStruct((1, ncond, tile_size), jnp.float32),
        [VMEM],
        scratch=[
            pltpu.VMEM((ncond, tile_size), jnp.float32),
            pltpu.SemaphoreType.DMA((4,)),
        ],
        nbytes=6 * ncond * tile_size,
        out_space=ANY,
        name="widen",
    )(tiles)


def solution(mesh):
    return jax.shard_map(
        per_device,
        mesh=mesh,
        in_specs=(
            P("grp", "cond"),
            P("cond", None),
            P(("grp", "cond"), None),
            P(("grp", "cond"), None),
            P(("grp", "cond"), None),
        ),
        out_specs=P(("grp", "cond"), None, None),
        check_vma=False,
    )
```

```python
import functools

import jax
import jax.numpy as jnp
from jax import lax
from jax.experimental import pallas as pl
from jax.experimental.pallas import tpu as pltpu
from jax.sharding import PartitionSpec as P

LANES = 128
CORES = 2
BLOCK = 16
EARLY, MAIN, FURTHER = 48, 104, (8, 16)
VMEM = pl.BlockSpec(memory_space=pltpu.VMEM)
ANY = pl.BlockSpec(memory_space=pl.ANY)
SMEM = pl.BlockSpec(memory_space=pltpu.SMEM)


def in_hbm(x):
    return pltpu.with_memory_space_constraint(x, pltpu.HBM)


def in_vmem(x):
    return pltpu.with_memory_space_constraint(x, pltpu.VMEM)


def exchanged(x, axes, groups=None):
    return lax.all_to_all(
        x, axes, split_axis=0, concat_axis=0, tiled=True, axis_index_groups=groups
    )


def from_other_core(x):
    count = lax.axis_size("grp")
    return lax.ppermute(x, "grp", [(i, i ^ 1) for i in range(count)])


def against(rows, other):
    return lax.dot_general(
        rows, other, (((1,), (1,)), ((), ())), preferred_element_type=jnp.float32
    )


def kernel_call(body, out_shape, in_specs, scratch=(), mib=16, flops=0, nbytes=0, out_space=VMEM, name=None):
    return pl.pallas_call(
        body,
        out_shape=out_shape,
        in_specs=in_specs,
        out_specs=out_space,
        scratch_shapes=scratch,
        compiler_params=pltpu.CompilerParams(vmem_limit_bytes=mib << 20),
        cost_estimate=pl.CostEstimate(flops=flops, bytes_accessed=nbytes, transcendentals=0),
        name=name,
    )


def core_half(own_half, width):
    core = lax.axis_index("grp") % CORES
    which = core if own_half else 1 - core
    return pl.ds(pl.multiple_of(which * width, width), width)


def load_body(
    valence_hbm, screened_hbm, counts_hbm, owner_hbm, valence_ref, screened_ref,
    blocks_ref, bases_ref, counts, owner, sems,
):
    lanes = core_half(True, screened_ref.shape[1])
    first = pltpu.make_async_copy(counts_hbm, counts, sems.at[0])
    copies = [
        pltpu.make_async_copy(screened_hbm.at[:, lanes], screened_ref, sems.at[1]),
        pltpu.make_async_copy(valence_hbm, valence_ref, sems.at[2]),
        pltpu.make_async_copy(owner_hbm, owner, sems.at[3]),
    ]
    first.start()
    for copy in copies:
        copy.start()
    ncond = counts.shape[1]
    blocks = (MAIN + sum(FURTHER)) // ncond
    for i in range(blocks_ref.shape[1]):
        blocks_ref[0, i] = 0
    first.wait()
    used = jnp.int32(0)
    for j in range(ncond):
        bases_ref[0, j] = used
        for i in range(blocks):
            blocks_ref[0, used + i] = j * blocks + i
        used = used + (counts[0, j] + (BLOCK - 1)) // BLOCK
    for i in range(blocks):
        blocks_ref[0, used + i] = 0
    bases_ref[0, ncond] = used
    for copy in copies:
        copy.wait()


def partial_body(own_ref, other_ref, screened_ref, out_ref):
    core = lax.axis_index("grp") % CORES
    half = screened_ref[...]
    rows = jnp.concatenate([own_ref[...], other_ref[...]], axis=0)
    both = jnp.dot(rows, half, preferred_element_type=jnp.float32)
    own, other = both[: own_ref.shape[0]], both[own_ref.shape[0] :]
    for t in range(half.shape[1] // LANES):
        lanes = slice(t * LANES, (t + 1) * LANES)
        out_ref[CORES * t + core] = own[:, lanes]
        out_ref[CORES * t + (1 - core)] = other[:, lanes]


def sum_body(pieces_ref, cond_ref, out_ref):
    total = pieces_ref[0]
    for c in range(1, pieces_ref.shape[0]):
        total = total + pieces_ref[c]
    rounded = total.astype(jnp.bfloat16)
    for d in range(out_ref.shape[0]):
        out_ref[d] = rounded


def assemble(groups, pieces_ref, projected):
    ncond = pieces_ref.shape[0] * CORES // groups
    rows_dev = pieces_ref.shape[1]
    valence_all = groups * rows_dev
    for d in range(pieces_ref.shape[0]):
        c = d % ncond
        group = CORES * (d // ncond) + c % CORES
        lanes = slice(c // CORES * LANES, (c // CORES + 1) * LANES)
        piece = pieces_ref[d]
        for start in (group * rows_dev, valence_all + group * rows_dev):
            projected[start : start + rows_dev, lanes] = piece


def rows_of(begin, end):
    return slice(begin * BLOCK, end * BLOCK)


def packed_product(begin, end, lanes, cond_ref, blocks_ref, projected):
    rows = [
        cond_ref[pl.ds(pl.multiple_of(blocks_ref[0, i] * BLOCK, BLOCK), BLOCK), lanes]
        for i in range(begin, end)
    ]
    return against(jnp.concatenate(rows, axis=0), projected[...])


def further_products(bases_ref, chunk):
    used = bases_ref[0, bases_ref.shape[1] - 1]
    begin = MAIN
    for count in FURTHER:
        pl.when(used > begin)(functools.partial(chunk, begin, begin + count))
        begin += count


def first_body(groups, pieces_ref, cond_ref, blocks_ref, bases_ref, out_ref, projected):
    assemble(groups, pieces_ref, projected)
    lanes = core_half(True, projected.shape[1])

    def chunk(begin, end):
        out_ref[rows_of(begin, end), :] = packed_product(
            begin, end, lanes, cond_ref, blocks_ref, projected
        )

    chunk(0, MAIN)
    further_products(bases_ref, chunk)


def tiles_body(
    groups, pieces_ref, cond_ref, first_ref, blocks_ref, bases_ref, counts, owner,
    out_ref, projected, early, total,
):
    assemble(groups, pieces_ref, projected)
    lanes = core_half(False, projected.shape[1])
    ncond, pairs, _ = out_ref.shape
    lane = lax.broadcasted_iota(jnp.int32, (pairs, LANES), 1)
    second = lane >= LANES // 2
    place = 2 * lax.broadcasted_iota(jnp.int32, (pairs, LANES), 0) + second.astype(jnp.int32)

    def chunk(begin, end):
        rows = rows_of(begin, end)
        total[rows, :] = first_ref[rows, :] + packed_product(
            begin, end, lanes, cond_ref, blocks_ref, projected
        )

    def put_tiles(source, tiles):
        for j in tiles:
            begin = pl.multiple_of(bases_ref[0, j] * BLOCK, BLOCK)
            even = source[pl.ds(begin, pairs, stride=2), :]
            odd = source[pl.ds(begin + 1, pairs, stride=2), :]
            tile = jnp.where(second, odd, even)
            tile = jnp.where(place < counts[0, j], tile, jnp.float32(0.0))
            out_ref[owner[0, j]] = tile.astype(jnp.bfloat16)

    rows = rows_of(0, EARLY)
    product = first_ref[rows, :] + packed_product(
        0, EARLY, lanes, cond_ref, blocks_ref, projected
    )
    early[rows, :] = product
    total[rows, :] = product
    chunk(EARLY, MAIN)
    safe = EARLY // (2 * pairs // BLOCK)
    put_tiles(early, range(safe))
    further_products(bases_ref, chunk)
    put_tiles(total, range(safe, ncond))


def widen_body(tiles_ref, out_ref, wide, sems):
    count, pairs, lanes = tiles_ref.shape
    copies = []
    for i in range(sems.shape[0]):
        rows = slice(i * count // sems.shape[0], (i + 1) * count // sems.shape[0])
        tiles = tiles_ref[rows].astype(jnp.float32)
        wide[rows, :] = tiles.reshape(tiles.shape[0], pairs * lanes)
        copies.append(
            pltpu.make_async_copy(wide.at[rows, :], out_ref.at[0, rows, :], sems.at[i])
        )
        copies[-1].start()
    for copy in copies:
        copy.wait()


def per_device(valence_pairs, screened, cond_pairs, owner_map, band_counts):
    groups = lax.axis_size("grp")
    ncond = lax.axis_size("cond")
    rows_dev = valence_pairs.shape[0]
    waves = screened.shape[1]
    pairs_dev = cond_pairs.shape[0]
    valence_all = groups * rows_dev
    tile_size = pairs_dev // ncond * valence_all
    pairs = tile_size // LANES
    same_core = [
        [g * ncond + c for g in range(core, groups, CORES) for c in range(ncond)]
        for core in range(CORES)
    ]

    tile_rows = pairs_dev // ncond
    own, screened_half, blocks, bases, counts, owner = kernel_call(
        load_body,
        [
            pltpu.VMEM(valence_pairs.shape, valence_pairs.dtype),
            pltpu.VMEM((screened.shape[0], waves // CORES), screened.dtype),
            pltpu.SMEM((1, pairs_dev // BLOCK + tile_rows // BLOCK), jnp.int32),
            pltpu.SMEM((1, ncond + 1), jnp.int32),
            pltpu.SMEM(band_counts.shape, band_counts.dtype),
            pltpu.SMEM(owner_map.shape, owner_map.dtype),
        ],
        [ANY, ANY, ANY, ANY],
        scratch=[pltpu.SemaphoreType.DMA((4,))],
        nbytes=2 * screened.size,
        out_space=[VMEM, VMEM, SMEM, SMEM, SMEM, SMEM],
        name="load_first",
    )(in_hbm(valence_pairs), in_hbm(screened), in_hbm(band_counts), in_hbm(owner_map))
    pieces = kernel_call(
        partial_body,
        jax.ShapeDtypeStruct((ncond, rows_dev, LANES), jnp.float32),
        [VMEM, VMEM, VMEM],
        flops=2 * rows_dev * screened.shape[0] * waves,
        nbytes=2 * screened.size,
        name="partial",
    )(
        in_vmem(own), from_other_core(valence_pairs), in_vmem(screened_half)
    )
    arrived = exchanged(pieces, "cond")
    copies = kernel_call(
        sum_body,
        jax.ShapeDtypeStruct((len(same_core[0]), rows_dev, LANES), jnp.bfloat16),
        [VMEM, ANY],
        nbytes=arrived.size * 4,
        name="sum_pieces",
    )(arrived, in_hbm(cond_pairs))
    gathered = exchanged(copies, ("grp", "cond"), same_core)
    others = from_other_core(gathered)
    half_scratch = [pltpu.VMEM((2 * valence_all, waves // CORES), jnp.bfloat16)]
    first = kernel_call(
        functools.partial(first_body, groups),
        jax.ShapeDtypeStruct((pairs_dev, LANES), jnp.float32),
        [VMEM, VMEM, SMEM, SMEM],
        scratch=half_scratch,
        flops=pairs_dev * waves * valence_all,
        nbytes=cond_pairs.size,
        name="first_half",
    )(gathered, cond_pairs, blocks, bases)
    outgoing = kernel_call(
        functools.partial(tiles_body, groups),
        jax.ShapeDtypeStruct((ncond, pairs, LANES), jnp.bfloat16),
        [VMEM, VMEM, VMEM, SMEM, SMEM, SMEM, SMEM],
        scratch=[
            *half_scratch,
            pltpu.VMEM((EARLY * BLOCK + tile_rows + BLOCK, LANES), jnp.float32),
            pltpu.VMEM((pairs_dev + tile_rows + BLOCK, LANES), jnp.float32),
        ],
        flops=pairs_dev * waves * valence_all,
        nbytes=cond_pairs.size,
        name="tiles",
    )(others, cond_pairs, first, blocks, bases, counts, owner)
    tiles = exchanged(outgoing, "cond")
    return kernel_call(
        widen_body,
        jax.ShapeDtypeStruct((1, ncond, tile_size), jnp.float32),
        [VMEM],
        scratch=[
            pltpu.VMEM((ncond, tile_size), jnp.float32),
            pltpu.SemaphoreType.DMA((4,)),
        ],
        nbytes=6 * ncond * tile_size,
        out_space=ANY,
        name="widen",
    )(tiles)


def solution(mesh):
    return jax.shard_map(
        per_device,
        mesh=mesh,
        in_specs=(
            P("grp", "cond"),
            P("cond", None),
            P(("grp", "cond"), None),
            P(("grp", "cond"), None),
            P(("grp", "cond"), None),
        ),
        out_specs=P(("grp", "cond"), None, None),
        check_vma=False,
    )
```

```python
import functools

import jax
import jax.numpy as jnp
from jax import lax
from jax.experimental import pallas as pl
from jax.experimental.pallas import tpu as pltpu
from jax.sharding import PartitionSpec as P

LANES = 128
CORES = 2
BLOCK = 16
EARLY, MAIN, FURTHER = 48, 104, (8, 16)
VMEM = pl.BlockSpec(memory_space=pltpu.VMEM)
ANY = pl.BlockSpec(memory_space=pl.ANY)
SMEM = pl.BlockSpec(memory_space=pltpu.SMEM)


def in_hbm(x):
    return pltpu.with_memory_space_constraint(x, pltpu.HBM)


def in_vmem(x):
    return pltpu.with_memory_space_constraint(x, pltpu.VMEM)


def exchanged(x, axes, groups=None):
    return lax.all_to_all(
        x, axes, split_axis=0, concat_axis=0, tiled=True, axis_index_groups=groups
    )


def from_other_core(x):
    count = lax.axis_size("grp")
    return lax.ppermute(x, "grp", [(i, i ^ 1) for i in range(count)])


def against(rows, other):
    return lax.dot_general(
        rows, other, (((1,), (1,)), ((), ())), preferred_element_type=jnp.float32
    )


def kernel_call(body, out_shape, in_specs, scratch=(), mib=16, flops=0, nbytes=0, out_space=VMEM, name=None):
    return pl.pallas_call(
        body,
        out_shape=out_shape,
        in_specs=in_specs,
        out_specs=out_space,
        scratch_shapes=scratch,
        compiler_params=pltpu.CompilerParams(vmem_limit_bytes=mib << 20),
        cost_estimate=pl.CostEstimate(flops=flops, bytes_accessed=nbytes, transcendentals=0),
        name=name,
    )


def core_half(own_half, width):
    core = lax.axis_index("grp") % CORES
    which = core if own_half else 1 - core
    return pl.ds(pl.multiple_of(which * width, width), width)


def load_body(
    valence_hbm, screened_hbm, counts_hbm, owner_hbm, valence_ref, screened_ref,
    blocks_ref, bases_ref, counts, owner, sems,
):
    lanes = core_half(True, screened_ref.shape[1])
    first = pltpu.make_async_copy(counts_hbm, counts, sems.at[0])
    copies = [
        pltpu.make_async_copy(screened_hbm.at[:, lanes], screened_ref, sems.at[1]),
        pltpu.make_async_copy(valence_hbm, valence_ref, sems.at[2]),
        pltpu.make_async_copy(owner_hbm, owner, sems.at[3]),
    ]
    first.start()
    for copy in copies:
        copy.start()
    ncond = counts.shape[1]
    blocks = (MAIN + sum(FURTHER)) // ncond
    for i in range(blocks_ref.shape[1]):
        blocks_ref[0, i] = 0
    first.wait()
    used = jnp.int32(0)
    for j in range(ncond):
        bases_ref[0, j] = used
        for i in range(blocks):
            blocks_ref[0, used + i] = j * blocks + i
        used = used + (counts[0, j] + (BLOCK - 1)) // BLOCK
    for i in range(blocks):
        blocks_ref[0, used + i] = 0
    bases_ref[0, ncond] = used
    for copy in copies:
        copy.wait()


def partial_body(own_ref, other_ref, screened_ref, out_ref):
    core = lax.axis_index("grp") % CORES
    half = screened_ref[...]
    rows = jnp.concatenate([own_ref[...], other_ref[...]], axis=0)
    both = jnp.dot(rows, half, preferred_element_type=jnp.float32)
    own, other = both[: own_ref.shape[0]], both[own_ref.shape[0] :]
    for t in range(half.shape[1] // LANES):
        lanes = slice(t * LANES, (t + 1) * LANES)
        out_ref[CORES * t + core] = own[:, lanes]
        out_ref[CORES * t + (1 - core)] = other[:, lanes]


def sum_body(pieces_ref, cond_ref, out_ref):
    total = pieces_ref[0]
    for c in range(1, pieces_ref.shape[0]):
        total = total + pieces_ref[c]
    rounded = total.astype(jnp.bfloat16)
    for d in range(out_ref.shape[0]):
        out_ref[d] = rounded


def assemble(groups, pieces_ref, projected):
    ncond = pieces_ref.shape[0] * CORES // groups
    rows_dev = pieces_ref.shape[1]
    valence_all = groups * rows_dev
    for d in range(pieces_ref.shape[0]):
        c = d % ncond
        group = CORES * (d // ncond) + c % CORES
        lanes = slice(c // CORES * LANES, (c // CORES + 1) * LANES)
        piece = pieces_ref[d]
        for start in (group * rows_dev, valence_all + group * rows_dev):
            projected[start : start + rows_dev, lanes] = piece


def rows_of(begin, end):
    return slice(begin * BLOCK, end * BLOCK)


def packed_product(begin, end, lanes, cond_ref, blocks_ref, projected):
    rows = [
        cond_ref[pl.ds(pl.multiple_of(blocks_ref[0, i] * BLOCK, BLOCK), BLOCK), lanes]
        for i in range(begin, end)
    ]
    return against(jnp.concatenate(rows, axis=0), projected[...])


def further_products(bases_ref, chunk):
    used = bases_ref[0, bases_ref.shape[1] - 1]
    begin = MAIN
    for count in FURTHER:
        pl.when(used > begin)(functools.partial(chunk, begin, begin + count))
        begin += count


def first_product(groups, pieces_ref, cond_ref, blocks_ref, bases_ref, out_ref, projected):
    assemble(groups, pieces_ref, projected)
    lanes = core_half(True, projected.shape[1])

    def chunk(begin, end):
        out_ref[rows_of(begin, end), :] = packed_product(
            begin, end, lanes, cond_ref, blocks_ref, projected
        )

    chunk(0, MAIN)
    further_products(bases_ref, chunk)


def early_body(groups, *refs):
    @pl.when(lax.axis_index("grp") % CORES == 1)
    def _():
        first_product(groups, *refs)


def first_body(groups, early_ref, pieces_ref, cond_ref, blocks_ref, bases_ref, out_ref, projected):
    core = lax.axis_index("grp") % CORES

    @pl.when(core == 1)
    def _():
        out_ref[...] = early_ref[...]

    @pl.when(core == 0)
    def _():
        first_product(groups, pieces_ref, cond_ref, blocks_ref, bases_ref, out_ref, projected)


def tiles_body(
    groups, pieces_ref, cond_ref, first_ref, blocks_ref, bases_ref, counts, owner,
    out_ref, projected, early, total,
):
    assemble(groups, pieces_ref, projected)
    lanes = core_half(False, projected.shape[1])
    ncond, pairs, _ = out_ref.shape
    lane = lax.broadcasted_iota(jnp.int32, (pairs, LANES), 1)
    second = lane >= LANES // 2
    place = 2 * lax.broadcasted_iota(jnp.int32, (pairs, LANES), 0) + second.astype(jnp.int32)

    def chunk(begin, end):
        rows = rows_of(begin, end)
        total[rows, :] = first_ref[rows, :] + packed_product(
            begin, end, lanes, cond_ref, blocks_ref, projected
        )

    def put_tiles(source, tiles):
        for j in tiles:
            begin = pl.multiple_of(bases_ref[0, j] * BLOCK, BLOCK)
            even = source[pl.ds(begin, pairs, stride=2), :]
            odd = source[pl.ds(begin + 1, pairs, stride=2), :]
            tile = jnp.where(second, odd, even)
            tile = jnp.where(place < counts[0, j], tile, jnp.float32(0.0))
            out_ref[owner[0, j]] = tile.astype(jnp.bfloat16)

    rows = rows_of(0, EARLY)
    product = first_ref[rows, :] + packed_product(
        0, EARLY, lanes, cond_ref, blocks_ref, projected
    )
    early[rows, :] = product
    total[rows, :] = product
    chunk(EARLY, MAIN)
    safe = EARLY // (2 * pairs // BLOCK)
    put_tiles(early, range(safe))
    further_products(bases_ref, chunk)
    put_tiles(total, range(safe, ncond))


def widen_body(tiles_ref, out_ref, wide, sems):
    count, pairs, lanes = tiles_ref.shape
    copies = []
    for i in range(sems.shape[0]):
        rows = slice(i * count // sems.shape[0], (i + 1) * count // sems.shape[0])
        tiles = tiles_ref[rows].astype(jnp.float32)
        wide[rows, :] = tiles.reshape(tiles.shape[0], pairs * lanes)
        copies.append(
            pltpu.make_async_copy(wide.at[rows, :], out_ref.at[0, rows, :], sems.at[i])
        )
        copies[-1].start()
    for copy in copies:
        copy.wait()


def per_device(valence_pairs, screened, cond_pairs, owner_map, band_counts):
    groups = lax.axis_size("grp")
    ncond = lax.axis_size("cond")
    rows_dev = valence_pairs.shape[0]
    waves = screened.shape[1]
    pairs_dev = cond_pairs.shape[0]
    valence_all = groups * rows_dev
    tile_size = pairs_dev // ncond * valence_all
    pairs = tile_size // LANES
    same_core = [
        [g * ncond + c for g in range(core, groups, CORES) for c in range(ncond)]
        for core in range(CORES)
    ]

    tile_rows = pairs_dev // ncond
    own, screened_half, blocks, bases, counts, owner = kernel_call(
        load_body,
        [
            pltpu.VMEM(valence_pairs.shape, valence_pairs.dtype),
            pltpu.VMEM((screened.shape[0], waves // CORES), screened.dtype),
            pltpu.SMEM((1, pairs_dev // BLOCK + tile_rows // BLOCK), jnp.int32),
            pltpu.SMEM((1, ncond + 1), jnp.int32),
            pltpu.SMEM(band_counts.shape, band_counts.dtype),
            pltpu.SMEM(owner_map.shape, owner_map.dtype),
        ],
        [ANY, ANY, ANY, ANY],
        scratch=[pltpu.SemaphoreType.DMA((4,))],
        nbytes=2 * screened.size,
        out_space=[VMEM, VMEM, SMEM, SMEM, SMEM, SMEM],
        name="load_first",
    )(in_hbm(valence_pairs), in_hbm(screened), in_hbm(band_counts), in_hbm(owner_map))
    pieces = kernel_call(
        partial_body,
        jax.ShapeDtypeStruct((ncond, rows_dev, LANES), jnp.float32),
        [VMEM, VMEM, VMEM],
        flops=2 * rows_dev * screened.shape[0] * waves,
        nbytes=2 * screened.size,
        name="partial",
    )(
        in_vmem(own), from_other_core(valence_pairs), in_vmem(screened_half)
    )
    arrived = exchanged(pieces, "cond")
    copies = kernel_call(
        sum_body,
        jax.ShapeDtypeStruct((len(same_core[0]), rows_dev, LANES), jnp.bfloat16),
        [VMEM, ANY],
        nbytes=arrived.size * 4,
        name="sum_pieces",
    )(arrived, in_hbm(cond_pairs))
    gathered = exchanged(copies, ("grp", "cond"), same_core)
    half_scratch = [pltpu.VMEM((2 * valence_all, waves // CORES), jnp.bfloat16)]
    half_product = jax.ShapeDtypeStruct((pairs_dev, LANES), jnp.float32)
    early = kernel_call(
        functools.partial(early_body, groups),
        half_product,
        [VMEM, VMEM, SMEM, SMEM],
        scratch=half_scratch,
        flops=pairs_dev * waves * valence_all,
        nbytes=cond_pairs.size,
        name="first_half_core1",
    )(gathered, cond_pairs, blocks, bases)
    gathered, early = lax.optimization_barrier((gathered, early))
    others = from_other_core(gathered)
    first = kernel_call(
        functools.partial(first_body, groups),
        half_product,
        [VMEM, VMEM, VMEM, SMEM, SMEM],
        scratch=half_scratch,
        flops=pairs_dev * waves * valence_all,
        nbytes=cond_pairs.size,
        name="first_half_core0",
    )(early, gathered, cond_pairs, blocks, bases)
    outgoing = kernel_call(
        functools.partial(tiles_body, groups),
        jax.ShapeDtypeStruct((ncond, pairs, LANES), jnp.bfloat16),
        [VMEM, VMEM, VMEM, SMEM, SMEM, SMEM, SMEM],
        scratch=[
            *half_scratch,
            pltpu.VMEM((EARLY * BLOCK + tile_rows + BLOCK, LANES), jnp.float32),
            pltpu.VMEM((pairs_dev + tile_rows + BLOCK, LANES), jnp.float32),
        ],
        flops=pairs_dev * waves * valence_all,
        nbytes=cond_pairs.size,
        name="tiles",
    )(others, cond_pairs, first, blocks, bases, counts, owner)
    tiles = exchanged(outgoing, "cond")
    return kernel_call(
        widen_body,
        jax.ShapeDtypeStruct((1, ncond, tile_size), jnp.float32),
        [VMEM],
        scratch=[
            pltpu.VMEM((ncond, tile_size), jnp.float32),
            pltpu.SemaphoreType.DMA((4,)),
        ],
        nbytes=6 * ncond * tile_size,
        out_space=ANY,
        name="widen",
    )(tiles)


def solution(mesh):
    return jax.shard_map(
        per_device,
        mesh=mesh,
        in_specs=(
            P("grp", "cond"),
            P("cond", None),
            P(("grp", "cond"), None),
            P(("grp", "cond"), None),
            P(("grp", "cond"), None),
        ),
        out_specs=P(("grp", "cond"), None, None),
        check_vma=False,
    )
```

```python
import functools

import jax
import jax.numpy as jnp
from jax import lax
from jax.experimental import pallas as pl
from jax.experimental.pallas import tpu as pltpu
from jax.sharding import PartitionSpec as P

LANES = 128
CORES = 2
ROOT = 22
BLOCK = 16
EARLY, MAIN, FURTHER = 48, 104, (8, 16)
VMEM = pl.BlockSpec(memory_space=pltpu.VMEM)
ANY = pl.BlockSpec(memory_space=pl.ANY)
SMEM = pl.BlockSpec(memory_space=pltpu.SMEM)


def in_hbm(x):
    return pltpu.with_memory_space_constraint(x, pltpu.HBM)


def in_vmem(x):
    return pltpu.with_memory_space_constraint(x, pltpu.VMEM)


def exchanged(x, axes, groups=None):
    return lax.all_to_all(
        x, axes, split_axis=0, concat_axis=0, tiled=True, axis_index_groups=groups
    )


def from_other_core(x):
    count = lax.axis_size("grp")
    return lax.ppermute(x, "grp", [(i, i ^ 1) for i in range(count)])


def against(rows, other):
    return lax.dot_general(
        rows, other, (((1,), (1,)), ((), ())), preferred_element_type=jnp.float32
    )


def kernel_call(body, out_shape, in_specs, scratch=(), mib=16, flops=0, nbytes=0, out_space=VMEM, name=None):
    return pl.pallas_call(
        body,
        out_shape=out_shape,
        in_specs=in_specs,
        out_specs=out_space,
        scratch_shapes=scratch,
        compiler_params=pltpu.CompilerParams(vmem_limit_bytes=mib << 20),
        cost_estimate=pl.CostEstimate(flops=flops, bytes_accessed=nbytes, transcendentals=0),
        name=name,
    )


def core_half(own_half, width):
    core = lax.axis_index("grp") % CORES
    which = core if own_half else 1 - core
    return pl.ds(pl.multiple_of(which * width, width), width)


def load_body(
    valence_hbm, screened_hbm, counts_hbm, owner_hbm, valence_ref, screened_ref,
    blocks_ref, bases_ref, counts, owner, sems,
):
    lanes = core_half(True, screened_ref.shape[1])
    first = pltpu.make_async_copy(counts_hbm, counts, sems.at[0])
    copies = [
        pltpu.make_async_copy(screened_hbm.at[:, lanes], screened_ref, sems.at[1]),
        pltpu.make_async_copy(valence_hbm, valence_ref, sems.at[2]),
        pltpu.make_async_copy(owner_hbm, owner, sems.at[3]),
    ]
    first.start()
    for copy in copies:
        copy.start()
    ncond = counts.shape[1]
    blocks = (MAIN + sum(FURTHER)) // ncond
    for i in range(blocks_ref.shape[1]):
        blocks_ref[0, i] = 0
    first.wait()
    used = jnp.int32(0)
    for j in range(ncond):
        bases_ref[0, j] = used
        for i in range(blocks):
            blocks_ref[0, used + i] = j * blocks + i
        used = used + (counts[0, j] + (BLOCK - 1)) // BLOCK
    for i in range(blocks):
        blocks_ref[0, used + i] = 0
    bases_ref[0, ncond] = used
    for copy in copies:
        copy.wait()


def partial_body(own_ref, other_ref, screened_ref, out_ref):
    core = lax.axis_index("grp") % CORES
    half = screened_ref[...]
    rows = jnp.concatenate([own_ref[...], other_ref[...]], axis=0)
    both = jnp.dot(rows, half, preferred_element_type=jnp.float32)
    own, other = both[: own_ref.shape[0]], both[own_ref.shape[0] :]
    for t in range(half.shape[1] // LANES):
        lanes = slice(t * LANES, (t + 1) * LANES)
        place = (CORES * t) ^ ROOT
        out_ref[place + core] = own[:, lanes]
        out_ref[place + (1 - core)] = other[:, lanes]


def sum_body(pieces_ref, cond_ref, out_ref):
    total = pieces_ref[0]
    for c in range(1, pieces_ref.shape[0]):
        total = total + pieces_ref[c]
    rounded = total.astype(jnp.bfloat16)
    for d in range(out_ref.shape[0]):
        out_ref[d] = rounded


def assemble(groups, pieces_ref, projected):
    ncond = pieces_ref.shape[0] * CORES // groups
    rows_dev = pieces_ref.shape[1]
    valence_all = groups * rows_dev
    for d in range(pieces_ref.shape[0]):
        c = (d % ncond) ^ ROOT
        group = CORES * (d // ncond) + c % CORES
        lanes = slice(c // CORES * LANES, (c // CORES + 1) * LANES)
        piece = pieces_ref[d]
        for start in (group * rows_dev, valence_all + group * rows_dev):
            projected[start : start + rows_dev, lanes] = piece


def rows_of(begin, end):
    return slice(begin * BLOCK, end * BLOCK)


def packed_product(begin, end, lanes, cond_ref, blocks_ref, projected):
    rows = [
        cond_ref[pl.ds(pl.multiple_of(blocks_ref[0, i] * BLOCK, BLOCK), BLOCK), lanes]
        for i in range(begin, end)
    ]
    return against(jnp.concatenate(rows, axis=0), projected[...])


def further_products(bases_ref, chunk):
    used = bases_ref[0, bases_ref.shape[1] - 1]
    begin = MAIN
    for count in FURTHER:
        pl.when(used > begin)(functools.partial(chunk, begin, begin + count))
        begin += count


def first_product(groups, pieces_ref, cond_ref, blocks_ref, bases_ref, out_ref, projected):
    assemble(groups, pieces_ref, projected)
    lanes = core_half(True, projected.shape[1])

    def chunk(begin, end):
        out_ref[rows_of(begin, end), :] = packed_product(
            begin, end, lanes, cond_ref, blocks_ref, projected
        )

    chunk(0, MAIN)
    further_products(bases_ref, chunk)


def early_body(groups, *refs):
    @pl.when(lax.axis_index("grp") % CORES == 1)
    def _():
        first_product(groups, *refs)


def first_body(groups, early_ref, pieces_ref, cond_ref, blocks_ref, bases_ref, out_ref, projected):
    core = lax.axis_index("grp") % CORES

    @pl.when(core == 1)
    def _():
        out_ref[...] = early_ref[...]

    @pl.when(core == 0)
    def _():
        first_product(groups, pieces_ref, cond_ref, blocks_ref, bases_ref, out_ref, projected)


def tiles_body(
    groups, pieces_ref, cond_ref, first_ref, blocks_ref, bases_ref, counts, owner,
    out_ref, projected, early, total,
):
    assemble(groups, pieces_ref, projected)
    lanes = core_half(False, projected.shape[1])
    ncond, pairs, _ = out_ref.shape
    lane = lax.broadcasted_iota(jnp.int32, (pairs, LANES), 1)
    second = lane >= LANES // 2
    place = 2 * lax.broadcasted_iota(jnp.int32, (pairs, LANES), 0) + second.astype(jnp.int32)

    def chunk(begin, end):
        rows = rows_of(begin, end)
        total[rows, :] = first_ref[rows, :] + packed_product(
            begin, end, lanes, cond_ref, blocks_ref, projected
        )

    def put_tiles(source, tiles):
        for j in tiles:
            begin = pl.multiple_of(bases_ref[0, j] * BLOCK, BLOCK)
            even = source[pl.ds(begin, pairs, stride=2), :]
            odd = source[pl.ds(begin + 1, pairs, stride=2), :]
            tile = jnp.where(second, odd, even)
            tile = jnp.where(place < counts[0, j], tile, jnp.float32(0.0))
            out_ref[owner[0, j] ^ ROOT] = tile.astype(jnp.bfloat16)

    rows = rows_of(0, EARLY)
    product = first_ref[rows, :] + packed_product(
        0, EARLY, lanes, cond_ref, blocks_ref, projected
    )
    early[rows, :] = product
    total[rows, :] = product
    chunk(EARLY, MAIN)
    safe = EARLY // (2 * pairs // BLOCK)
    put_tiles(early, range(safe))
    further_products(bases_ref, chunk)
    put_tiles(total, range(safe, ncond))


def widen_body(tiles_ref, out_ref, wide, sems):
    count, pairs, lanes = tiles_ref.shape
    copies = []
    for i in range(sems.shape[0]):
        rows = slice(i * count // sems.shape[0], (i + 1) * count // sems.shape[0])
        order = [tiles_ref[s ^ ROOT] for s in range(rows.start, rows.stop)]
        tiles = jnp.stack(order).astype(jnp.float32)
        wide[rows, :] = tiles.reshape(tiles.shape[0], pairs * lanes)
        copies.append(
            pltpu.make_async_copy(wide.at[rows, :], out_ref.at[0, rows, :], sems.at[i])
        )
        copies[-1].start()
    for copy in copies:
        copy.wait()


def per_device(valence_pairs, screened, cond_pairs, owner_map, band_counts):
    groups = lax.axis_size("grp")
    ncond = lax.axis_size("cond")
    rows_dev = valence_pairs.shape[0]
    waves = screened.shape[1]
    pairs_dev = cond_pairs.shape[0]
    valence_all = groups * rows_dev
    tile_size = pairs_dev // ncond * valence_all
    pairs = tile_size // LANES
    order = [p ^ ROOT for p in range(ncond)]
    same_grp = [[g * ncond + c for c in order] for g in range(groups)]
    same_core = [
        [g * ncond + c for g in range(core, groups, CORES) for c in order]
        for core in range(CORES)
    ]

    tile_rows = pairs_dev // ncond
    own, screened_half, blocks, bases, counts, owner = kernel_call(
        load_body,
        [
            pltpu.VMEM(valence_pairs.shape, valence_pairs.dtype),
            pltpu.VMEM((screened.shape[0], waves // CORES), screened.dtype),
            pltpu.SMEM((1, pairs_dev // BLOCK + tile_rows // BLOCK), jnp.int32),
            pltpu.SMEM((1, ncond + 1), jnp.int32),
            pltpu.SMEM(band_counts.shape, band_counts.dtype),
            pltpu.SMEM(owner_map.shape, owner_map.dtype),
        ],
        [ANY, ANY, ANY, ANY],
        scratch=[pltpu.SemaphoreType.DMA((4,))],
        nbytes=2 * screened.size,
        out_space=[VMEM, VMEM, SMEM, SMEM, SMEM, SMEM],
        name="load_first",
    )(in_hbm(valence_pairs), in_hbm(screened), in_hbm(band_counts), in_hbm(owner_map))
    pieces = kernel_call(
        partial_body,
        jax.ShapeDtypeStruct((ncond, rows_dev, LANES), jnp.float32),
        [VMEM, VMEM, VMEM],
        flops=2 * rows_dev * screened.shape[0] * waves,
        nbytes=2 * screened.size,
        name="partial",
    )(
        in_vmem(own), from_other_core(valence_pairs), in_vmem(screened_half)
    )
    arrived = exchanged(pieces, ("grp", "cond"), same_grp)
    copies = kernel_call(
        sum_body,
        jax.ShapeDtypeStruct((len(same_core[0]), rows_dev, LANES), jnp.bfloat16),
        [VMEM, ANY],
        nbytes=arrived.size * 4,
        name="sum_pieces",
    )(arrived, in_hbm(cond_pairs))
    gathered = exchanged(copies, ("grp", "cond"), same_core)
    half_scratch = [pltpu.VMEM((2 * valence_all, waves // CORES), jnp.bfloat16)]
    half_product = jax.ShapeDtypeStruct((pairs_dev, LANES), jnp.float32)
    early = kernel_call(
        functools.partial(early_body, groups),
        half_product,
        [VMEM, VMEM, SMEM, SMEM],
        scratch=half_scratch,
        flops=pairs_dev * waves * valence_all,
        nbytes=cond_pairs.size,
        name="first_half_core1",
    )(gathered, cond_pairs, blocks, bases)
    gathered, early = lax.optimization_barrier((gathered, early))
    others = from_other_core(gathered)
    first = kernel_call(
        functools.partial(first_body, groups),
        half_product,
        [VMEM, VMEM, VMEM, SMEM, SMEM],
        scratch=half_scratch,
        flops=pairs_dev * waves * valence_all,
        nbytes=cond_pairs.size,
        name="first_half_core0",
    )(early, gathered, cond_pairs, blocks, bases)
    outgoing = kernel_call(
        functools.partial(tiles_body, groups),
        jax.ShapeDtypeStruct((ncond, pairs, LANES), jnp.bfloat16),
        [VMEM, VMEM, VMEM, SMEM, SMEM, SMEM, SMEM],
        scratch=[
            *half_scratch,
            pltpu.VMEM((EARLY * BLOCK + tile_rows + BLOCK, LANES), jnp.float32),
            pltpu.VMEM((pairs_dev + tile_rows + BLOCK, LANES), jnp.float32),
        ],
        flops=pairs_dev * waves * valence_all,
        nbytes=cond_pairs.size,
        name="tiles",
    )(others, cond_pairs, first, blocks, bases, counts, owner)
    tiles = exchanged(outgoing, ("grp", "cond"), same_grp)
    return kernel_call(
        widen_body,
        jax.ShapeDtypeStruct((1, ncond, tile_size), jnp.float32),
        [VMEM],
        scratch=[
            pltpu.VMEM((ncond, tile_size), jnp.float32),
            pltpu.SemaphoreType.DMA((4,)),
        ],
        nbytes=6 * ncond * tile_size,
        out_space=ANY,
        name="widen",
    )(tiles)


def solution(mesh):
    return jax.shard_map(
        per_device,
        mesh=mesh,
        in_specs=(
            P("grp", "cond"),
            P("cond", None),
            P(("grp", "cond"), None),
            P(("grp", "cond"), None),
            P(("grp", "cond"), None),
        ),
        out_specs=P(("grp", "cond"), None, None),
        check_vma=False,
    )
```

```python
import functools

import jax
import jax.numpy as jnp
from jax import lax
from jax.experimental import pallas as pl
from jax.experimental.pallas import tpu as pltpu
from jax.sharding import PartitionSpec as P

LANES = 128
CORES = 2
ROOT = 22
BLOCK = 16
EARLY, MAIN, FURTHER = 48, 100, (4, 8, 16)
VMEM = pl.BlockSpec(memory_space=pltpu.VMEM)
ANY = pl.BlockSpec(memory_space=pl.ANY)
SMEM = pl.BlockSpec(memory_space=pltpu.SMEM)


def in_hbm(x):
    return pltpu.with_memory_space_constraint(x, pltpu.HBM)


def in_vmem(x):
    return pltpu.with_memory_space_constraint(x, pltpu.VMEM)


def exchanged(x, axes, groups=None):
    return lax.all_to_all(
        x, axes, split_axis=0, concat_axis=0, tiled=True, axis_index_groups=groups
    )


def from_other_core(x):
    count = lax.axis_size("grp")
    return lax.ppermute(x, "grp", [(i, i ^ 1) for i in range(count)])


def against(rows, other):
    return lax.dot_general(
        rows, other, (((1,), (1,)), ((), ())), preferred_element_type=jnp.float32
    )


def kernel_call(body, out_shape, in_specs, scratch=(), mib=16, flops=0, nbytes=0, out_space=VMEM, name=None):
    return pl.pallas_call(
        body,
        out_shape=out_shape,
        in_specs=in_specs,
        out_specs=out_space,
        scratch_shapes=scratch,
        compiler_params=pltpu.CompilerParams(vmem_limit_bytes=mib << 20),
        cost_estimate=pl.CostEstimate(flops=flops, bytes_accessed=nbytes, transcendentals=0),
        name=name,
    )


def core_half(own_half, width):
    core = lax.axis_index("grp") % CORES
    which = core if own_half else 1 - core
    return pl.ds(pl.multiple_of(which * width, width), width)


def load_body(
    valence_hbm, screened_hbm, counts_hbm, owner_hbm, valence_ref, screened_ref,
    blocks_ref, bases_ref, counts, owner, sems,
):
    lanes = core_half(True, screened_ref.shape[1])
    first = pltpu.make_async_copy(counts_hbm, counts, sems.at[0])
    copies = [
        pltpu.make_async_copy(screened_hbm.at[:, lanes], screened_ref, sems.at[1]),
        pltpu.make_async_copy(valence_hbm, valence_ref, sems.at[2]),
        pltpu.make_async_copy(owner_hbm, owner, sems.at[3]),
    ]
    first.start()
    for copy in copies:
        copy.start()
    ncond = counts.shape[1]
    blocks = (MAIN + sum(FURTHER)) // ncond
    for i in range(blocks_ref.shape[1]):
        blocks_ref[0, i] = 0
    first.wait()
    used = jnp.int32(0)
    for j in range(ncond):
        bases_ref[0, j] = used
        for i in range(blocks):
            blocks_ref[0, used + i] = j * blocks + i
        used = used + (counts[0, j] + (BLOCK - 1)) // BLOCK
    for i in range(blocks):
        blocks_ref[0, used + i] = 0
    bases_ref[0, ncond] = used
    for copy in copies:
        copy.wait()


def partial_body(own_ref, other_ref, screened_ref, out_ref):
    core = lax.axis_index("grp") % CORES
    half = screened_ref[...]
    rows = jnp.concatenate([own_ref[...], other_ref[...]], axis=0)
    both = jnp.dot(rows, half, preferred_element_type=jnp.float32)
    own, other = both[: own_ref.shape[0]], both[own_ref.shape[0] :]
    for t in range(half.shape[1] // LANES):
        lanes = slice(t * LANES, (t + 1) * LANES)
        place = (CORES * t) ^ ROOT
        out_ref[place + core] = own[:, lanes]
        out_ref[place + (1 - core)] = other[:, lanes]


def sum_body(pieces_ref, cond_ref, out_ref):
    total = pieces_ref[0]
    for c in range(1, pieces_ref.shape[0]):
        total = total + pieces_ref[c]
    rounded = total.astype(jnp.bfloat16)
    for d in range(out_ref.shape[0]):
        out_ref[d] = rounded


def assemble(groups, pieces_ref, projected):
    ncond = pieces_ref.shape[0] * CORES // groups
    rows_dev = pieces_ref.shape[1]
    valence_all = groups * rows_dev
    for d in range(pieces_ref.shape[0]):
        c = (d % ncond) ^ ROOT
        group = CORES * (d // ncond) + c % CORES
        lanes = slice(c // CORES * LANES, (c // CORES + 1) * LANES)
        piece = pieces_ref[d]
        for start in (group * rows_dev, valence_all + group * rows_dev):
            projected[start : start + rows_dev, lanes] = piece


def rows_of(begin, end):
    return slice(begin * BLOCK, end * BLOCK)


def packed_product(begin, end, lanes, cond_ref, blocks_ref, projected):
    rows = [
        cond_ref[pl.ds(pl.multiple_of(blocks_ref[0, i] * BLOCK, BLOCK), BLOCK), lanes]
        for i in range(begin, end)
    ]
    return against(jnp.concatenate(rows, axis=0), projected[...])


def further_products(bases_ref, chunk):
    used = bases_ref[0, bases_ref.shape[1] - 1]
    begin = MAIN
    for count in FURTHER:
        pl.when(used > begin)(functools.partial(chunk, begin, begin + count))
        begin += count


def first_product(groups, pieces_ref, cond_ref, blocks_ref, bases_ref, out_ref, projected):
    assemble(groups, pieces_ref, projected)
    lanes = core_half(True, projected.shape[1])

    def chunk(begin, end):
        out_ref[rows_of(begin, end), :] = packed_product(
            begin, end, lanes, cond_ref, blocks_ref, projected
        )

    chunk(0, MAIN)
    further_products(bases_ref, chunk)


def early_body(groups, *refs):
    @pl.when(lax.axis_index("grp") % CORES == 1)
    def _():
        first_product(groups, *refs)


def first_body(groups, early_ref, pieces_ref, cond_ref, blocks_ref, bases_ref, out_ref, projected):
    core = lax.axis_index("grp") % CORES

    @pl.when(core == 1)
    def _():
        out_ref[...] = early_ref[...]

    @pl.when(core == 0)
    def _():
        first_product(groups, pieces_ref, cond_ref, blocks_ref, bases_ref, out_ref, projected)


def tiles_body(
    groups, pieces_ref, cond_ref, first_ref, blocks_ref, bases_ref, counts, owner,
    out_ref, projected, early, total,
):
    assemble(groups, pieces_ref, projected)
    lanes = core_half(False, projected.shape[1])
    ncond, pairs, _ = out_ref.shape
    lane = lax.broadcasted_iota(jnp.int32, (pairs, LANES), 1)
    second = lane >= LANES // 2
    place = 2 * lax.broadcasted_iota(jnp.int32, (pairs, LANES), 0) + second.astype(jnp.int32)

    def chunk(begin, end):
        rows = rows_of(begin, end)
        total[rows, :] = first_ref[rows, :] + packed_product(
            begin, end, lanes, cond_ref, blocks_ref, projected
        )

    def put_tiles(source, tiles):
        for j in tiles:
            begin = pl.multiple_of(bases_ref[0, j] * BLOCK, BLOCK)
            even = source[pl.ds(begin, pairs, stride=2), :]
            odd = source[pl.ds(begin + 1, pairs, stride=2), :]
            tile = jnp.where(second, odd, even)
            tile = jnp.where(place < counts[0, j], tile, jnp.float32(0.0))
            out_ref[owner[0, j] ^ ROOT] = tile.astype(jnp.bfloat16)

    rows = rows_of(0, EARLY)
    product = first_ref[rows, :] + packed_product(
        0, EARLY, lanes, cond_ref, blocks_ref, projected
    )
    early[rows, :] = product
    total[rows, :] = product
    chunk(EARLY, MAIN)
    safe = EARLY // (2 * pairs // BLOCK)
    put_tiles(early, range(safe))
    further_products(bases_ref, chunk)
    put_tiles(total, range(safe, ncond))


def widen_body(tiles_ref, out_ref, wide, sems):
    count, pairs, lanes = tiles_ref.shape
    copies = []
    for i in range(sems.shape[0]):
        rows = slice(i * count // sems.shape[0], (i + 1) * count // sems.shape[0])
        order = [tiles_ref[s ^ ROOT] for s in range(rows.start, rows.stop)]
        tiles = jnp.stack(order).astype(jnp.float32)
        wide[rows, :] = tiles.reshape(tiles.shape[0], pairs * lanes)
        copies.append(
            pltpu.make_async_copy(wide.at[rows, :], out_ref.at[0, rows, :], sems.at[i])
        )
        copies[-1].start()
    for copy in copies:
        copy.wait()


def per_device(valence_pairs, screened, cond_pairs, owner_map, band_counts):
    groups = lax.axis_size("grp")
    ncond = lax.axis_size("cond")
    rows_dev = valence_pairs.shape[0]
    waves = screened.shape[1]
    pairs_dev = cond_pairs.shape[0]
    valence_all = groups * rows_dev
    tile_size = pairs_dev // ncond * valence_all
    pairs = tile_size // LANES
    order = [p ^ ROOT for p in range(ncond)]
    same_grp = [[g * ncond + c for c in order] for g in range(groups)]
    same_core = [
        [g * ncond + c for g in range(core, groups, CORES) for c in order]
        for core in range(CORES)
    ]

    tile_rows = pairs_dev // ncond
    own, screened_half, blocks, bases, counts, owner = kernel_call(
        load_body,
        [
            pltpu.VMEM(valence_pairs.shape, valence_pairs.dtype),
            pltpu.VMEM((screened.shape[0], waves // CORES), screened.dtype),
            pltpu.SMEM((1, pairs_dev // BLOCK + tile_rows // BLOCK), jnp.int32),
            pltpu.SMEM((1, ncond + 1), jnp.int32),
            pltpu.SMEM(band_counts.shape, band_counts.dtype),
            pltpu.SMEM(owner_map.shape, owner_map.dtype),
        ],
        [ANY, ANY, ANY, ANY],
        scratch=[pltpu.SemaphoreType.DMA((4,))],
        nbytes=2 * screened.size,
        out_space=[VMEM, VMEM, SMEM, SMEM, SMEM, SMEM],
        name="load_first",
    )(in_hbm(valence_pairs), in_hbm(screened), in_hbm(band_counts), in_hbm(owner_map))
    pieces = kernel_call(
        partial_body,
        jax.ShapeDtypeStruct((ncond, rows_dev, LANES), jnp.float32),
        [VMEM, VMEM, VMEM],
        flops=2 * rows_dev * screened.shape[0] * waves,
        nbytes=2 * screened.size,
        name="partial",
    )(
        in_vmem(own), from_other_core(valence_pairs), in_vmem(screened_half)
    )
    arrived = exchanged(pieces, ("grp", "cond"), same_grp)
    copies = kernel_call(
        sum_body,
        jax.ShapeDtypeStruct((len(same_core[0]), rows_dev, LANES), jnp.bfloat16),
        [VMEM, ANY],
        nbytes=arrived.size * 4,
        name="sum_pieces",
    )(arrived, in_hbm(cond_pairs))
    gathered = exchanged(copies, ("grp", "cond"), same_core)
    half_scratch = [pltpu.VMEM((2 * valence_all, waves // CORES), jnp.bfloat16)]
    half_product = jax.ShapeDtypeStruct((pairs_dev, LANES), jnp.float32)
    early = kernel_call(
        functools.partial(early_body, groups),
        half_product,
        [VMEM, VMEM, SMEM, SMEM],
        scratch=half_scratch,
        flops=pairs_dev * waves * valence_all,
        nbytes=cond_pairs.size,
        name="first_half_core1",
    )(gathered, cond_pairs, blocks, bases)
    gathered, early = lax.optimization_barrier((gathered, early))
    others = from_other_core(gathered)
    first = kernel_call(
        functools.partial(first_body, groups),
        half_product,
        [VMEM, VMEM, VMEM, SMEM, SMEM],
        scratch=half_scratch,
        flops=pairs_dev * waves * valence_all,
        nbytes=cond_pairs.size,
        name="first_half_core0",
    )(early, gathered, cond_pairs, blocks, bases)
    outgoing = kernel_call(
        functools.partial(tiles_body, groups),
        jax.ShapeDtypeStruct((ncond, pairs, LANES), jnp.bfloat16),
        [VMEM, VMEM, VMEM, SMEM, SMEM, SMEM, SMEM],
        scratch=[
            *half_scratch,
            pltpu.VMEM((EARLY * BLOCK + tile_rows + BLOCK, LANES), jnp.float32),
            pltpu.VMEM((pairs_dev + tile_rows + BLOCK, LANES), jnp.float32),
        ],
        flops=pairs_dev * waves * valence_all,
        nbytes=cond_pairs.size,
        name="tiles",
    )(others, cond_pairs, first, blocks, bases, counts, owner)
    tiles = exchanged(outgoing, ("grp", "cond"), same_grp)
    return kernel_call(
        widen_body,
        jax.ShapeDtypeStruct((1, ncond, tile_size), jnp.float32),
        [VMEM],
        scratch=[
            pltpu.VMEM((ncond, tile_size), jnp.float32),
            pltpu.SemaphoreType.DMA((4,)),
        ],
        nbytes=6 * ncond * tile_size,
        out_space=ANY,
        name="widen",
    )(tiles)


def solution(mesh):
    return jax.shard_map(
        per_device,
        mesh=mesh,
        in_specs=(
            P("grp", "cond"),
            P("cond", None),
            P(("grp", "cond"), None),
            P(("grp", "cond"), None),
            P(("grp", "cond"), None),
        ),
        out_specs=P(("grp", "cond"), None, None),
        check_vma=False,
    )
```
